32 devices in a mesh: groups: 2 (over y), dp: 4 (over z), feat: 2 (over x), node: 2 (over core).
Axes of the slice: x: 2, y: 2, z: 4, core: 2. Of those that a mesh axis runs over, the one named last changes fastest.
Arguments:
- bins: int32 [256, 32768], P('feat', ('groups', 'dp')), parts along dimension 1, may hold values from 0 to 255
- node_ids: int32 [32768], P(('groups', 'dp')), parts along dimension 0, may hold values from 0 to 63
- grad: bfloat16 [32768], P(('groups', 'dp')), parts along dimension 0, may hold values from -1 to 1
- hess: bfloat16 [32768], P(('groups', 'dp')), parts along dimension 0, may hold values from 0.019897461 to 0.25
Outputs:
- gains: float32 [128, 256, 256], P(('groups', 'node'), ('feat', 'dp')), parts along dimension 0
- best: float32 [128], P(('groups', 'node')), parts along dimension 0
The draws below stay inside these ranges and needn't reach their ends.
There are 2 independent parts, one for each index of `groups`. The reference program is written for one: setup_inputs(seed, part) draws one part's arguments, and reference() takes and returns one part's arrays. A program takes and returns all parts, laid end to end along the dimension named above; each array names one. Nothing has to cross between parts.
All inputs are finite; a program needn't handle non-finite values.
Results may differ from the reference program's by a relative error of at most 0.0003.
Values sent between devices are 32-bit elements; how exact they have to be, the bound alone decides.
A program may use at most 64 MiB of HBM per device.

```python
import math
import jax
import jax.numpy as jnp
from jax import lax

F = 256
BINS = 256
NODES = 64
ROWS = 16384


def plant(array, stream_key, low, top_value):
    longest = array.shape.index(max(array.shape))
    spots = []
    for shift in (0, 1):
        where = [jax.random.randint(jax.random.fold_in(stream_key, axis), (), 0, length) for axis, length in enumerate(array.shape)]
        where[longest] = (where[longest] + shift) % array.shape[longest]
        spots.append(tuple(where))
    return array.at[spots[0]].set(low).at[spots[1]].set(top_value)


def block_levels(key, shape, cuts, smallest, high):
    gain, own = 1.0, jax.random.fold_in(key, 6)
    for dim, parts in cuts:
        heights = jnp.exp(jax.random.uniform(jax.random.fold_in(own, dim), (parts,), jnp.float32, smallest / len(cuts), high / len(cuts)))
        gain = gain * jnp.repeat(heights, shape[dim] // parts).reshape([-1 if axis == dim else 1 for axis in range(len(shape))])
    return gain


def setup_inputs(seed: int = 0, part: int = 0) -> dict:
    seeds = jax.random.split(jax.random.key(seed), 5)
    part_keys = jax.random.split(jax.random.fold_in(seeds[4], part), 5)
    return {
        "bins": plant(jax.random.randint(part_keys[0], (F, ROWS), 0, BINS), jax.random.fold_in(part_keys[0], 1), 0, BINS - 1).astype(jnp.int32),
        "node_ids": plant(jax.random.randint(part_keys[1], (ROWS,), 0, NODES), jax.random.fold_in(part_keys[1], 1), 0, NODES - 1).astype(jnp.int32),
        "grad": jnp.clip(jax.random.uniform(part_keys[2], (ROWS,), jnp.float32, -1.0, 1.0) * block_levels(part_keys[2], (ROWS,), ((0, 4),), -0.4, 0.0), -1.0, 1.0).astype(jnp.bfloat16),
        "hess": jnp.clip(jnp.exp(math.log(0.25) - 2.5308688 * jax.random.uniform(part_keys[3], (ROWS,), jnp.float32) ** block_levels(part_keys[3], (ROWS,), ((0, 4),), -0.2, 0.2)), 0.019897461, 0.25).astype(jnp.bfloat16),
    }


LAMBDA_REG = 1.0


def reference(bins, node_ids, grad, hess):
    stats = jnp.stack([grad.astype(jnp.float32), hess.astype(jnp.float32)], 1)

    def feature_hist(column):
        segment = node_ids * BINS + column
        summed = jax.ops.segment_sum(stats, segment, num_segments=NODES * BINS)
        return summed.reshape(NODES, BINS, 2)

    hist = lax.map(feature_hist, bins)
    hist = jnp.transpose(hist, (1, 0, 2, 3))
    totals = jax.ops.segment_sum(stats, node_ids, num_segments=NODES)
    cumulated = jnp.cumsum(hist, axis=2)
    grad_left = cumulated[..., 0]
    hess_left = cumulated[..., 1]
    grad_total = totals[:, 0][:, None, None]
    hess_total = totals[:, 1][:, None, None]
    gains = 0.5 * (grad_left * grad_left / (hess_left + LAMBDA_REG)
                   + (grad_total - grad_left) ** 2 / (hess_total - hess_left + LAMBDA_REG)
                   - grad_total * grad_total / (hess_total + LAMBDA_REG))
    best = jnp.max(gains, axis=(1, 2))
    return gains, best
```

```python
import functools
import math

import jax
import jax.numpy as jnp
from jax import lax
from jax.experimental import pallas as pl
from jax.experimental.pallas import tpu as pltpu
from jax.sharding import PartitionSpec as P

BINS = 256
NODES = 64
LAMBDA_REG = 1.0
MESH = pl.DeviceIdType.MESH
CHUNK = 512


def flip(index, mask, size):
    result, bit = 0, 1
    while bit < size:
        value = (index // bit) % 2
        result = result + bit * ((1 - value) if mask & bit else value)
        bit *= 2
    return result


def partner(index, step, size):
    if size & (size - 1) == 0:
        return flip(index, step, size)
    return (step - index + size) % size


def kernel(
    sizes, bins_ref, aux_ref, gains_ref, best_ref,
    recv, aux, weights, left, ready, row, rows_dp, rows_all,
    local_sem, send_bins, recv_bins, send_aux, recv_aux,
    out_sem, send_out, recv_out, send_dp, recv_dp, send_all, recv_all,
):
    dp, feat, node = sizes
    half, row_count = recv.shape[1:]
    node_count = NODES // node
    z, x, c = lax.axis_index("dp"), lax.axis_index("feat"), lax.axis_index("node")
    group = math.gcd(half, 4)
    others = [(i, k) for i in range(feat) for k in range(node) if (i, k) != (0, 0)]

    def place(i, k):
        return {"feat": (x + i) % feat, "node": (c + k) % node}

    own_bins = pltpu.make_async_copy(bins_ref.at[z, c], recv.at[0], local_sem.at[0])
    own_aux = pltpu.make_async_copy(aux_ref, aux.at[0], local_sem.at[1])
    own_aux.start()
    own_bins.start()

    barrier = pltpu.get_barrier_semaphore()
    for step in range(1, dp):
        pl.semaphore_signal(
            barrier, inc=1, device_id={"dp": partner(z, step, dp)}, device_id_type=MESH
        )
    for i, k in others:
        pl.semaphore_signal(barrier, inc=1, device_id=place(i, k), device_id_type=MESH)
    pl.semaphore_wait(barrier, dp - 1 + len(others))

    copies = []
    for step in range(1, dp):
        to = partner(z, step, dp)
        for source, target, sent, received in (
            (aux_ref, aux, send_aux, recv_aux),
            (bins_ref.at[to, c], recv, send_bins, recv_bins),
        ):
            copy = pltpu.make_async_remote_copy(
                src_ref=source,
                dst_ref=target.at[step],
                send_sem=sent.at[step],
                recv_sem=received.at[step],
                device_id={"dp": to},
                device_id_type=MESH,
            )
            copy.start()
            copies.append(copy)

    ids = lax.broadcasted_iota(jnp.int32, (NODES, CHUNK), 0) + c * node_count
    ids = jnp.where(ids >= NODES, ids - NODES, ids).astype(jnp.float32)
    levels = lax.broadcasted_iota(jnp.int32, (BINS, CHUNK), 0).astype(jnp.float32)
    levels = levels.astype(jnp.bfloat16)

    def one_shard(step, first):
        @pl.loop(0, row_count // CHUNK)
        def _(block):
            span = pl.ds(pl.multiple_of(block * CHUNK, CHUNK), CHUNK)
            mine = aux[step, 0:1, span] == ids
            grad = jnp.where(mine, aux[step, 1:2, span], 0.0)
            hess = jnp.where(mine, aux[step, 2:3, span], 0.0)
            weights[span, :] = jnp.concatenate([grad, hess], 0).astype(jnp.bfloat16).T

        @pl.loop(0, half // group)
        def _(part):
            total = None
            for block in range(row_count // CHUNK):
                span = pl.ds(block * CHUNK, CHUNK)
                pieces = []
                for u in range(group):
                    values = recv[step, pl.ds(part * group + u, 1), span]
                    values = values.astype(jnp.float32).astype(jnp.bfloat16)
                    below = jnp.broadcast_to(values, (BINS, CHUNK)) <= levels
                    pieces.append(jnp.where(below, jnp.bfloat16(1), jnp.bfloat16(0)))
                product = jnp.dot(
                    jnp.concatenate(pieces, 0), weights[span, :], preferred_element_type=jnp.float32
                )
                total = product if total is None else total + product
            sums = total.reshape(group, BINS, 2 * NODES)
            where = pl.ds(part * group, group)
            if first:
                left[where] = sums
            else:
                left[where] += sums

    own_aux.wait()
    own_bins.wait()
    one_shard(0, True)

    @pl.loop(1, dp)
    def _(step):
        for source, target, received in (
            (aux_ref, aux, recv_aux),
            (bins_ref.at[0, 0], recv, recv_bins),
        ):
            pltpu.make_async_copy(source, target.at[step], received.at[step]).wait()
        one_shard(step, False)

    def one_feature(index, largest):
        table = left[index].T
        grad_left, hess_left = table[:NODES], table[NODES:]
        grad_total = grad_left[:, BINS - 1 :]
        hess_total = hess_left[:, BINS - 1 :]
        grad_right = grad_total - grad_left
        gains = 0.5 * (
            grad_left * grad_left / (hess_left + LAMBDA_REG)
            + grad_right * grad_right / (hess_total - hess_left + LAMBDA_REG)
            - grad_total * grad_total / (hess_total + LAMBDA_REG)
        )
        ready[:, pl.ds(index, 1), :] = gains.reshape(NODES, 1, BINS)
        return jnp.maximum(largest, jnp.maximum(gains[:, :128], gains[:, 128:]))

    largest = jnp.full((NODES, 128), -jnp.inf, jnp.float32)
    largest = lax.fori_loop(0, half, one_feature, largest)

    own_out = pltpu.make_async_copy(
        ready.at[pl.ds(0, node_count)], gains_ref.at[:, c], out_sem.at[0]
    )
    own_out.start()
    for k in range(1, node):
        copy = pltpu.make_async_remote_copy(
            src_ref=ready.at[pl.ds(k * node_count, node_count)],
            dst_ref=gains_ref.at[:, c],
            send_sem=send_out.at[k],
            recv_sem=recv_out.at[k],
            device_id={"node": (c + k) % node},
            device_id_type=MESH,
        )
        copy.start()
        copies.append(copy)

    best = jnp.max(largest.T, axis=0, keepdims=True)
    row[0, :, 0:NODES] = jnp.broadcast_to(best, (8, NODES))
    row[0, :, NODES:] = jnp.zeros((8, 128 - NODES), jnp.float32)
    sends = []
    for step in range(1, dp):
        copy = pltpu.make_async_remote_copy(
            src_ref=row.at[0],
            dst_ref=rows_dp.at[step],
            send_sem=send_dp.at[step],
            recv_sem=recv_dp.at[step],
            device_id={"dp": partner(z, step, dp)},
            device_id_type=MESH,
        )
        copy.start()
        sends.append(copy)
    best = row[0]
    for step in range(1, dp):
        sends[step - 1].wait_recv()
        best = jnp.maximum(best, rows_dp[step])
    row[1] = best
    last = []
    for number, (i, k) in enumerate(others):
        copy = pltpu.make_async_remote_copy(
            src_ref=row.at[1],
            dst_ref=rows_all.at[number],
            send_sem=send_all.at[number],
            recv_sem=recv_all.at[number],
            device_id=place(i, k),
            device_id_type=MESH,
        )
        copy.start()
        last.append(copy)
    best = best[:, :node_count]
    for number, (i, k) in enumerate(others):
        last[number].wait_recv()
        best = jnp.maximum(
            best, rows_all[number][:, k * node_count : (k + 1) * node_count]
        )
    best_ref[...] = best

    for copy in copies + sends + last:
        copy.wait_send()
    own_out.wait()
    for k in range(1, node):
        pltpu.make_async_copy(
            ready.at[pl.ds(0, node_count)], gains_ref.at[:, (c + node - k) % node], recv_out.at[k]
        ).wait()


def on_device(sizes, bins, node_ids, grad, hess):
    dp, feat, node = sizes
    feature_block, row_count = bins.shape
    half = feature_block // (dp * node)
    node_count = NODES // node
    aux = jnp.stack(
        [node_ids.astype(jnp.float32), grad.astype(jnp.float32), hess.astype(jnp.float32)], 0
    )
    split = bins.reshape(dp, node, half, row_count)
    peers = max(feat * node - 1, 1)
    dma = pltpu.SemaphoreType.DMA
    gains, best = pl.pallas_call(
        functools.partial(kernel, sizes),
        out_shape=(
            jax.ShapeDtypeStruct((node_count, node, half, BINS), jnp.float32),
            jax.ShapeDtypeStruct((8, node_count), jnp.float32),
        ),
        in_specs=[pl.BlockSpec(memory_space=pl.ANY)] * 2,
        out_specs=(
            pl.BlockSpec(memory_space=pl.ANY),
            pl.BlockSpec(memory_space=pltpu.VMEM),
        ),
        scratch_shapes=[
            pltpu.VMEM((dp, half, row_count), jnp.int32),
            pltpu.VMEM((dp, 3, row_count), jnp.float32),
            pltpu.VMEM((row_count, 2 * NODES), jnp.bfloat16),
            pltpu.VMEM((half, BINS, 2 * NODES), jnp.float32),
            pltpu.VMEM((NODES, half, BINS), jnp.float32),
            pltpu.VMEM((2, 8, 128), jnp.float32),
            pltpu.VMEM((dp, 8, 128), jnp.float32),
            pltpu.VMEM((peers, 8, 128), jnp.float32),
            dma((2,)),
            dma((dp,)), dma((dp,)), dma((dp,)), dma((dp,)),
            dma((1,)), dma((node,)), dma((node,)),
            dma((dp,)), dma((dp,)), dma((peers,)), dma((peers,)),
        ],
        compiler_params=pltpu.CompilerParams(
            collective_id=0, has_side_effects=True, vmem_limit_bytes=40 * 2**20
        ),
        name="split_gains",
    )(split, aux)
    return gains.reshape(node_count, node * half, BINS), best[0]


def solution(mesh):
    sizes = tuple(mesh.shape[axis] for axis in ("dp", "feat", "node"))
    return jax.shard_map(
        functools.partial(on_device, sizes),
        mesh=mesh,
        in_specs=(
            P("feat", ("groups", "dp")),
            P(("groups", "dp")),
            P(("groups", "dp")),
            P(("groups", "dp")),
        ),
        out_specs=(P(("groups", "node"), ("feat", "dp"), None), P(("groups", "node"))),
        check_vma=False,
    )
```

```python
import functools
import math

import jax
import jax.numpy as jnp
from jax import lax
from jax.experimental import pallas as pl
from jax.experimental.pallas import tpu as pltpu
from jax.sharding import PartitionSpec as P

BINS = 256
NODES = 64
LAMBDA_REG = 1.0
MESH = pl.DeviceIdType.MESH
CHUNK = 512


def flip(index, mask, size):
    result, bit = 0, 1
    while bit < size:
        value = (index // bit) % 2
        result = result + bit * ((1 - value) if mask & bit else value)
        bit *= 2
    return result


def partner(index, step, size):
    if size & (size - 1) == 0:
        return flip(index, step, size)
    return (step - index + size) % size


def kernel(
    sizes, bins_ref, aux_ref, gains_ref, best_ref,
    recv, aux, weights, left, ready, row, rows_dp, rows_all,
    local_sem, send_bins, recv_bins, send_aux, recv_aux,
    out_sem, send_out, recv_out, send_dp, recv_dp, send_all, recv_all,
):
    dp, feat, node = sizes
    half, row_count = recv.shape[1:]
    node_count = NODES // node
    z, x, c = lax.axis_index("dp"), lax.axis_index("feat"), lax.axis_index("node")
    group = math.gcd(half, 4)
    parts = half // group
    others = [(i, k) for i in range(feat) for k in range(node) if (i, k) != (0, 0)]

    def place(i, k):
        return {"feat": (x + i) % feat, "node": (c + k) % node}

    own_bins = pltpu.make_async_copy(bins_ref.at[z, c], recv.at[0], local_sem.at[0])
    own_aux = pltpu.make_async_copy(aux_ref, aux.at[0], local_sem.at[1])
    own_aux.start()
    own_bins.start()

    barrier = pltpu.get_barrier_semaphore()
    for step in range(1, dp):
        pl.semaphore_signal(
            barrier, inc=1, device_id={"dp": partner(z, step, dp)}, device_id_type=MESH
        )
    for i, k in others:
        pl.semaphore_signal(barrier, inc=1, device_id=place(i, k), device_id_type=MESH)
    ids = lax.broadcasted_iota(jnp.int32, (NODES, CHUNK), 0) + c * node_count
    ids = jnp.where(ids >= NODES, ids - NODES, ids).astype(jnp.float32)
    levels = lax.broadcasted_iota(jnp.int32, (BINS, CHUNK), 0).astype(jnp.float32)
    levels = levels.astype(jnp.bfloat16)

    def build(step):
        for block in range(row_count // CHUNK):
            span = pl.ds(block * CHUNK, CHUNK)
            mine = aux[step, 0:1, span] == ids
            grad = jnp.where(mine, aux[step, 1:2, span], 0.0)
            hess = jnp.where(mine, aux[step, 2:3, span], 0.0)
            weights[span, :] = jnp.concatenate([grad, hess], 0).astype(jnp.bfloat16).T

    own_aux.wait()
    build(0)
    pl.semaphore_wait(barrier, dp - 1 + len(others))

    copies = []
    for step in range(1, dp):
        to = partner(z, step, dp)
        for source, target, sent, received in (
            (aux_ref, aux, send_aux, recv_aux),
            (bins_ref.at[to, c], recv, send_bins, recv_bins),
        ):
            copy = pltpu.make_async_remote_copy(
                src_ref=source,
                dst_ref=target.at[step],
                send_sem=sent.at[step],
                recv_sem=received.at[step],
                device_id={"dp": to},
                device_id_type=MESH,
            )
            copy.start()
            copies.append(copy)

    def add_rows(step, part, first):
        total = None
        for block in range(row_count // CHUNK):
            span = pl.ds(block * CHUNK, CHUNK)
            pieces = []
            for u in range(group):
                values = recv[step, pl.ds(part * group + u, 1), span]
                values = values.astype(jnp.float32).astype(jnp.bfloat16)
                below = jnp.broadcast_to(values, (BINS, CHUNK)) <= levels
                pieces.append(jnp.where(below, jnp.bfloat16(1), jnp.bfloat16(0)))
            product = jnp.dot(
                jnp.concatenate(pieces, 0), weights[span, :], preferred_element_type=jnp.float32
            )
            total = product if total is None else total + product
        sums = total.reshape(group, BINS, 2 * NODES)
        where = pl.ds(part * group, group)
        if first:
            left[where] = sums
        else:
            left[where] += sums

    own_bins.wait()

    @pl.loop(0, parts)
    def _(part):
        add_rows(0, part, True)

    def arrive(step):
        for source, target, received in (
            (aux_ref, aux, recv_aux),
            (bins_ref.at[0, 0], recv, recv_bins),
        ):
            pltpu.make_async_copy(source, target.at[step], received.at[step]).wait()
        build(step)

    @pl.loop(1, dp - 1)
    def _(step):
        arrive(step)

        @pl.loop(0, parts)
        def _(part):
            add_rows(step, part, False)

    def one_feature(index, largest):
        table = left[index].T
        grad_left, hess_left = table[:NODES], table[NODES:]
        grad_total = grad_left[:, BINS - 1 :]
        hess_total = hess_left[:, BINS - 1 :]
        grad_right = grad_total - grad_left
        gains = 0.5 * (
            grad_left * grad_left / (hess_left + LAMBDA_REG)
            + grad_right * grad_right / (hess_total - hess_left + LAMBDA_REG)
            - grad_total * grad_total / (hess_total + LAMBDA_REG)
        )
        ready[:, pl.ds(index, 1), :] = gains.reshape(NODES, 1, BINS)
        return jnp.maximum(largest, jnp.maximum(gains[:, :128], gains[:, 128:]))

    def finish(part, largest):
        for u in range(group):
            largest = one_feature(part * group + u, largest)
        return largest

    def finish_and_add(part, largest):
        largest = finish(part - 1, largest)
        add_rows(dp - 1, part, False)
        return largest

    def hand_out(number, start, size):
        span = pl.ds(start, size)
        copy = pltpu.make_async_copy(
            ready.at[pl.ds(0, node_count), span], gains_ref.at[:, c, span], out_sem.at[number]
        )
        copy.start()
        outs.append(copy)
        for k in range(1, node):
            copy = pltpu.make_async_remote_copy(
                src_ref=ready.at[pl.ds(k * node_count, node_count), span],
                dst_ref=gains_ref.at[:, c, span],
                send_sem=send_out.at[number, k],
                recv_sem=recv_out.at[number, k],
                device_id={"node": (c + k) % node},
                device_id_type=MESH,
            )
            copy.start()
            copies.append(copy)

    outs = []
    early = (half - group) // 8 * 8
    largest = jnp.full((NODES, 128), -jnp.inf, jnp.float32)
    arrive(dp - 1)
    add_rows(dp - 1, 0, False)
    largest = lax.fori_loop(1, parts, finish_and_add, largest)
    if early:
        hand_out(0, 0, early)
    largest = finish(parts - 1, largest)
    hand_out(1, early, half - early)

    best = jnp.max(largest.T, axis=0, keepdims=True)
    row[0, :, 0:NODES] = jnp.broadcast_to(best, (8, NODES))
    row[0, :, NODES:] = jnp.zeros((8, 128 - NODES), jnp.float32)
    sends = []
    for step in range(1, dp):
        copy = pltpu.make_async_remote_copy(
            src_ref=row.at[0],
            dst_ref=rows_dp.at[step],
            send_sem=send_dp.at[step],
            recv_sem=recv_dp.at[step],
            device_id={"dp": partner(z, step, dp)},
            device_id_type=MESH,
        )
        copy.start()
        sends.append(copy)
    best = row[0]
    for step in range(1, dp):
        sends[step - 1].wait_recv()
        best = jnp.maximum(best, rows_dp[step])
    row[1] = best
    last = []
    for number, (i, k) in enumerate(others):
        copy = pltpu.make_async_remote_copy(
            src_ref=row.at[1],
            dst_ref=rows_all.at[number],
            send_sem=send_all.at[number],
            recv_sem=recv_all.at[number],
            device_id=place(i, k),
            device_id_type=MESH,
        )
        copy.start()
        last.append(copy)
    best = best[:, :node_count]
    for number, (i, k) in enumerate(others):
        last[number].wait_recv()
        best = jnp.maximum(
            best, rows_all[number][:, k * node_count : (k + 1) * node_count]
        )
    best_ref[...] = best

    for copy in copies + sends + last:
        copy.wait_send()
    for copy in outs:
        copy.wait()
    for number, start, size in ((0, 0, early), (1, early, half - early)):
        for k in range(1, node):
            if size:
                span = pl.ds(start, size)
                pltpu.make_async_copy(
                    ready.at[pl.ds(0, node_count), span],
                    gains_ref.at[:, (c + node - k) % node, span],
                    recv_out.at[number, k],
                ).wait()


def on_device(sizes, bins, node_ids, grad, hess):
    dp, feat, node = sizes
    feature_block, row_count = bins.shape
    half = feature_block // (dp * node)
    node_count = NODES // node
    line = lax.broadcasted_iota(jnp.int32, (3, row_count), 0)
    aux = jnp.where(
        line == 0,
        node_ids.astype(jnp.float32)[None],
        jnp.where(line == 1, grad.astype(jnp.float32)[None], hess.astype(jnp.float32)[None]),
    )
    split = bins.reshape(dp, node, half, row_count)
    peers = max(feat * node - 1, 1)
    dma = pltpu.SemaphoreType.DMA
    gains, best = pl.pallas_call(
        functools.partial(kernel, sizes),
        out_shape=(
            jax.ShapeDtypeStruct((node_count, node, half, BINS), jnp.float32),
            jax.ShapeDtypeStruct((8, node_count), jnp.float32),
        ),
        in_specs=[pl.BlockSpec(memory_space=pltpu.HBM), pl.BlockSpec(memory_space=pl.ANY)],
        out_specs=(
            pl.BlockSpec(memory_space=pl.ANY),
            pl.BlockSpec(memory_space=pltpu.VMEM),
        ),
        scratch_shapes=[
            pltpu.VMEM((dp, half, row_count), jnp.int32),
            pltpu.VMEM((dp, 3, row_count), jnp.float32),
            pltpu.VMEM((row_count, 2 * NODES), jnp.bfloat16),
            pltpu.VMEM((half, BINS, 2 * NODES), jnp.float32),
            pltpu.VMEM((NODES, half, BINS), jnp.float32),
            pltpu.VMEM((2, 8, 128), jnp.float32),
            pltpu.VMEM((dp, 8, 128), jnp.float32),
            pltpu.VMEM((peers, 8, 128), jnp.float32),
            dma((2,)),
            dma((dp,)), dma((dp,)), dma((dp,)), dma((dp,)),
            dma((2,)), dma((2, node)), dma((2, node)),
            dma((dp,)), dma((dp,)), dma((peers,)), dma((peers,)),
        ],
        compiler_params=pltpu.CompilerParams(
            collective_id=0, has_side_effects=True, vmem_limit_bytes=56 * 2**20
        ),
        name="split_gains",
    )(split, aux)
    return gains.reshape(node_count, node * half, BINS), best[0]


def solution(mesh):
    sizes = tuple(mesh.shape[axis] for axis in ("dp", "feat", "node"))
    return jax.shard_map(
        functools.partial(on_device, sizes),
        mesh=mesh,
        in_specs=(
            P("feat", ("groups", "dp")),
            P(("groups", "dp")),
            P(("groups", "dp")),
            P(("groups", "dp")),
        ),
        out_specs=(P(("groups", "node"), ("feat", "dp"), None), P(("groups", "node"))),
        check_vma=False,
    )
```

```python
import functools
import math

import jax
import jax.numpy as jnp
from jax import lax
from jax.experimental import pallas as pl
from jax.experimental.pallas import tpu as pltpu
from jax.sharding import PartitionSpec as P

BINS = 256
NODES = 64
LAMBDA_REG = 1.0
MESH = pl.DeviceIdType.MESH
CHUNK = 512


def flip(index, mask, size):
    result, bit = 0, 1
    while bit < size:
        value = (index // bit) % 2
        result = result + bit * ((1 - value) if mask & bit else value)
        bit *= 2
    return result


def partner(index, step, size):
    if size & (size - 1) == 0:
        return flip(index, step, size)
    return (step - index + size) % size


def kernel(
    sizes, bins_ref, aux_ref, gains_ref, best_ref,
    recv, aux, weights, left, ready, row, rows_dp, rows_all,
    local_sem, send_bins, recv_bins, send_aux, recv_aux,
    out_sem, send_out, recv_out, send_dp, recv_dp, send_all, recv_all,
):
    dp, feat, node = sizes
    half, row_count = recv.shape[1:]
    node_count = NODES // node
    z, x, c = lax.axis_index("dp"), lax.axis_index("feat"), lax.axis_index("node")
    group = math.gcd(half, 8)
    parts = half // group
    others = [(i, k) for i in range(feat) for k in range(node) if (i, k) != (0, 0)]

    def place(i, k):
        return {"feat": (x + i) % feat, "node": (c + k) % node}

    own_bins = pltpu.make_async_copy(bins_ref.at[z, c], recv.at[0], local_sem.at[0])
    own_aux = pltpu.make_async_copy(aux_ref, aux.at[0], local_sem.at[1])
    own_aux.start()
    own_bins.start()

    barrier = pltpu.get_barrier_semaphore()
    for step in range(1, dp):
        pl.semaphore_signal(
            barrier, inc=1, device_id={"dp": partner(z, step, dp)}, device_id_type=MESH
        )
    for i, k in others:
        pl.semaphore_signal(barrier, inc=1, device_id=place(i, k), device_id_type=MESH)
    ids = lax.broadcasted_iota(jnp.int32, (NODES, CHUNK), 0) + c * node_count
    ids = jnp.where(ids >= NODES, ids - NODES, ids).astype(jnp.float32)
    levels = lax.broadcasted_iota(jnp.int32, (BINS, CHUNK), 0).astype(jnp.float32)
    levels = levels.astype(jnp.bfloat16)

    def build(step):
        for block in range(row_count // CHUNK):
            span = pl.ds(block * CHUNK, CHUNK)
            mine = aux[step, 0:1, span] == ids
            grad = jnp.where(mine, aux[step, 1:2, span], 0.0)
            hess = jnp.where(mine, aux[step, 2:3, span], 0.0)
            weights[span, :] = jnp.concatenate([grad, hess], 0).astype(jnp.bfloat16).T

    pl.semaphore_wait(barrier, dp - 1 + len(others))

    copies = []
    for step in range(1, dp):
        to = partner(z, step, dp)
        for source, target, sent, received in (
            (aux_ref, aux, send_aux, recv_aux),
            (bins_ref.at[to, c], recv, send_bins, recv_bins),
        ):
            copy = pltpu.make_async_remote_copy(
                src_ref=source,
                dst_ref=target.at[step],
                send_sem=sent.at[step],
                recv_sem=received.at[step],
                device_id={"dp": to},
                device_id_type=MESH,
            )
            copy.start()
            copies.append(copy)

    def add_rows(step, part, first):
        total = None
        for block in range(row_count // CHUNK):
            span = pl.ds(block * CHUNK, CHUNK)
            pieces = []
            for u in range(group):
                values = recv[step, pl.ds(part * group + u, 1), span]
                values = values.astype(jnp.float32).astype(jnp.bfloat16)
                below = jnp.broadcast_to(values, (BINS, CHUNK)) <= levels
                pieces.append(jnp.where(below, jnp.bfloat16(1), jnp.bfloat16(0)))
            product = jnp.dot(
                jnp.concatenate(pieces, 0), weights[span, :], preferred_element_type=jnp.float32
            )
            total = product if total is None else total + product
        sums = total.reshape(group, BINS, 2 * NODES)
        where = pl.ds(part * group, group)
        if first:
            left[where] = sums
        else:
            left[where] += sums

    own_aux.wait()
    build(0)
    own_bins.wait()

    @pl.loop(0, parts)
    def _(part):
        add_rows(0, part, True)

    def arrive(step):
        for source, target, received in (
            (aux_ref, aux, recv_aux),
            (bins_ref.at[0, 0], recv, recv_bins),
        ):
            pltpu.make_async_copy(source, target.at[step], received.at[step]).wait()
        build(step)

    @pl.loop(1, dp - 1)
    def _(step):
        arrive(step)

        @pl.loop(0, parts)
        def _(part):
            add_rows(step, part, False)

    def one_feature(index, largest):
        table = left[index].T
        grad_left, hess_left = table[:NODES], table[NODES:]
        grad_total = grad_left[:, BINS - 1 :]
        hess_total = hess_left[:, BINS - 1 :]
        grad_right = grad_total - grad_left
        gains = 0.5 * (
            grad_left * grad_left / (hess_left + LAMBDA_REG)
            + grad_right * grad_right / (hess_total - hess_left + LAMBDA_REG)
            - grad_total * grad_total / (hess_total + LAMBDA_REG)
        )
        ready[:, pl.ds(index, 1), :] = gains.reshape(NODES, 1, BINS)
        return jnp.maximum(largest, jnp.maximum(gains[:, :128], gains[:, 128:]))

    def finish(part, largest):
        for u in range(group):
            largest = one_feature(part * group + u, largest)
        return largest

    def finish_and_add(part, largest):
        largest = finish(part - 1, largest)
        add_rows(dp - 1, part, False)
        return largest

    def hand_out(number, start, size):
        span = pl.ds(start, size)
        copy = pltpu.make_async_copy(
            ready.at[pl.ds(0, node_count), span], gains_ref.at[:, c, span], out_sem.at[number]
        )
        copy.start()
        outs.append(copy)
        for k in range(1, node):
            copy = pltpu.make_async_remote_copy(
                src_ref=ready.at[pl.ds(k * node_count, node_count), span],
                dst_ref=gains_ref.at[:, c, span],
                send_sem=send_out.at[number, k],
                recv_sem=recv_out.at[number, k],
                device_id={"node": (c + k) % node},
                device_id_type=MESH,
            )
            copy.start()
            copies.append(copy)

    outs = []
    early = (half - group) // 8 * 8
    largest = jnp.full((NODES, 128), -jnp.inf, jnp.float32)
    arrive(dp - 1)
    add_rows(dp - 1, 0, False)
    largest = lax.fori_loop(1, parts, finish_and_add, largest)
    if early:
        hand_out(0, 0, early)
    largest = finish(parts - 1, largest)
    hand_out(1, early, half - early)

    best = jnp.max(largest.T, axis=0, keepdims=True)
    row[0, :, 0:NODES] = jnp.broadcast_to(best, (8, NODES))
    row[0, :, NODES:] = jnp.zeros((8, 128 - NODES), jnp.float32)
    sends = []
    for step in range(1, dp):
        copy = pltpu.make_async_remote_copy(
            src_ref=row.at[0],
            dst_ref=rows_dp.at[step],
            send_sem=send_dp.at[step],
            recv_sem=recv_dp.at[step],
            device_id={"dp": partner(z, step, dp)},
            device_id_type=MESH,
        )
        copy.start()
        sends.append(copy)
    best = row[0]
    for step in range(1, dp):
        sends[step - 1].wait_recv()
        best = jnp.maximum(best, rows_dp[step])
    row[1] = best
    last = []
    for number, (i, k) in enumerate(others):
        copy = pltpu.make_async_remote_copy(
            src_ref=row.at[1],
            dst_ref=rows_all.at[number],
            send_sem=send_all.at[number],
            recv_sem=recv_all.at[number],
            device_id=place(i, k),
            device_id_type=MESH,
        )
        copy.start()
        last.append(copy)
    best = best[:, :node_count]
    for number, (i, k) in enumerate(others):
        last[number].wait_recv()
        best = jnp.maximum(
            best, rows_all[number][:, k * node_count : (k + 1) * node_count]
        )
    best_ref[...] = best

    for copy in copies + sends + last:
        copy.wait_send()
    for copy in outs:
        copy.wait()
    for number, start, size in ((0, 0, early), (1, early, half - early)):
        for k in range(1, node):
            if size:
                span = pl.ds(start, size)
                pltpu.make_async_copy(
                    ready.at[pl.ds(0, node_count), span],
                    gains_ref.at[:, (c + node - k) % node, span],
                    recv_out.at[number, k],
                ).wait()


def on_device(sizes, bins, node_ids, grad, hess):
    dp, feat, node = sizes
    feature_block, row_count = bins.shape
    half = feature_block // (dp * node)
    node_count = NODES // node
    line = lax.broadcasted_iota(jnp.int32, (3, row_count), 0)
    aux = jnp.where(
        line == 0,
        node_ids.astype(jnp.float32)[None],
        jnp.where(line == 1, grad.astype(jnp.float32)[None], hess.astype(jnp.float32)[None]),
    )
    split = bins.reshape(dp, node, half, row_count)
    peers = max(feat * node - 1, 1)
    dma = pltpu.SemaphoreType.DMA
    gains, best = pl.pallas_call(
        functools.partial(kernel, sizes),
        out_shape=(
            jax.ShapeDtypeStruct((node_count, node, half, BINS), jnp.float32),
            jax.ShapeDtypeStruct((8, node_count), jnp.float32),
        ),
        in_specs=[pl.BlockSpec(memory_space=pltpu.HBM), pl.BlockSpec(memory_space=pl.ANY)],
        out_specs=(
            pl.BlockSpec(memory_space=pl.ANY),
            pl.BlockSpec(memory_space=pltpu.VMEM),
        ),
        scratch_shapes=[
            pltpu.VMEM((dp, half, row_count), jnp.int32),
            pltpu.VMEM((dp, 3, row_count), jnp.float32),
            pltpu.VMEM((row_count, 2 * NODES), jnp.bfloat16),
            pltpu.VMEM((half, BINS, 2 * NODES), jnp.float32),
            pltpu.VMEM((NODES, half, BINS), jnp.float32),
            pltpu.VMEM((2, 8, 128), jnp.float32),
            pltpu.VMEM((dp, 8, 128), jnp.float32),
            pltpu.VMEM((peers, 8, 128), jnp.float32),
            dma((2,)),
            dma((dp,)), dma((dp,)), dma((dp,)), dma((dp,)),
            dma((2,)), dma((2, node)), dma((2, node)),
            dma((dp,)), dma((dp,)), dma((peers,)), dma((peers,)),
        ],
        compiler_params=pltpu.CompilerParams(
            collective_id=0, has_side_effects=True, vmem_limit_bytes=40 * 2**20
        ),
        name="split_gains",
    )(split, aux)
    return gains.reshape(node_count, node * half, BINS), best[0]


def solution(mesh):
    sizes = tuple(mesh.shape[axis] for axis in ("dp", "feat", "node"))
    return jax.shard_map(
        functools.partial(on_device, sizes),
        mesh=mesh,
        in_specs=(
            P("feat", ("groups", "dp")),
            P(("groups", "dp")),
            P(("groups", "dp")),
            P(("groups", "dp")),
        ),
        out_specs=(P(("groups", "node"), ("feat", "dp"), None), P(("groups", "node"))),
        check_vma=False,
    )
```

```python
import functools
import math

import jax
import jax.numpy as jnp
from jax import lax
from jax.experimental import pallas as pl
from jax.experimental.pallas import tpu as pltpu
from jax.sharding import PartitionSpec as P

BINS = 256
NODES = 64
LAMBDA_REG = 1.0
MESH = pl.DeviceIdType.MESH
CHUNK = 512


def flip(index, mask, size):
    result, bit = 0, 1
    while bit < size:
        value = (index // bit) % 2
        result = result + bit * ((1 - value) if mask & bit else value)
        bit *= 2
    return result


def partner(index, step, size):
    if size & (size - 1) == 0:
        return flip(index, step, size)
    return (step - index + size) % size


def kernel(
    sizes, bins_ref, aux_ref, gains_ref, best_ref,
    recv, aux, weights, left, ready, row, rows_dp, rows_all,
    local_sem, send_bins, recv_bins, send_aux, recv_aux,
    out_sem, send_out, recv_out, send_dp, recv_dp, send_all, recv_all,
):
    dp, feat, node = sizes
    half, row_count = recv.shape[1:]
    node_count = NODES // node
    z, x, c = lax.axis_index("dp"), lax.axis_index("feat"), lax.axis_index("node")
    group = math.gcd(half, 8)
    parts = half // group
    others = [(i, k) for i in range(feat) for k in range(node) if (i, k) != (0, 0)]

    def place(i, k):
        return {"feat": (x + i) % feat, "node": (c + k) % node}

    own_bins = pltpu.make_async_copy(bins_ref.at[z, c], recv.at[0], local_sem.at[0])
    own_aux = pltpu.make_async_copy(aux_ref, aux.at[0], local_sem.at[1])
    own_aux.start()
    own_bins.start()

    barrier = pltpu.get_barrier_semaphore()
    for step in range(1, dp):
        pl.semaphore_signal(
            barrier, inc=1, device_id={"dp": partner(z, step, dp)}, device_id_type=MESH
        )
    for i, k in others:
        pl.semaphore_signal(barrier, inc=1, device_id=place(i, k), device_id_type=MESH)
    ids = lax.broadcasted_iota(jnp.int32, (NODES, CHUNK), 0) + c * node_count
    ids = jnp.where(ids >= NODES, ids - NODES, ids).astype(jnp.float32)
    levels = lax.broadcasted_iota(jnp.int32, (BINS, CHUNK), 0).astype(jnp.float32)
    levels = levels.astype(jnp.bfloat16)

    def build(step):
        for block in range(row_count // CHUNK):
            span = pl.ds(block * CHUNK, CHUNK)
            mine = aux[step, 0:1, span] == ids
            grad = jnp.where(mine, aux[step, 1:2, span], 0.0)
            hess = jnp.where(mine, aux[step, 2:3, span], 0.0)
            weights[span, :] = jnp.concatenate([grad, hess], 0).astype(jnp.bfloat16).T

    pl.semaphore_wait(barrier, dp - 1 + len(others))

    copies = []
    for step in range(1, dp):
        to = partner(z, step, dp)
        for source, target, sent, received in (
            (aux_ref, aux, send_aux, recv_aux),
            (bins_ref.at[to, c], recv, send_bins, recv_bins),
        ):
            copy = pltpu.make_async_remote_copy(
                src_ref=source,
                dst_ref=target.at[step],
                send_sem=sent.at[step],
                recv_sem=received.at[step],
                device_id={"dp": to},
                device_id_type=MESH,
            )
            copy.start()
            copies.append(copy)

    def add_rows(step, part, first):
        total = None
        for block in range(row_count // CHUNK):
            span = pl.ds(block * CHUNK, CHUNK)
            pieces = []
            for u in range(group):
                values = recv[step, pl.ds(part * group + u, 1), span]
                values = values.astype(jnp.float32).astype(jnp.bfloat16)
                below = jnp.broadcast_to(values, (BINS, CHUNK)) <= levels
                pieces.append(jnp.where(below, jnp.bfloat16(1), jnp.bfloat16(0)))
            product = jnp.dot(
                jnp.concatenate(pieces, 0), weights[span, :], preferred_element_type=jnp.float32
            )
            total = product if total is None else total + product
        sums = total.reshape(group, BINS, 2 * NODES)
        where = pl.ds(part * group, group)
        if first:
            left[where] = sums
        else:
            left[where] += sums

    own_aux.wait()
    build(0)
    own_bins.wait()

    @pl.loop(0, parts)
    def _(part):
        add_rows(0, part, True)

    def arrive(step):
        for source, target, received in (
            (aux_ref, aux, recv_aux),
            (bins_ref.at[0, 0], recv, recv_bins),
        ):
            pltpu.make_async_copy(source, target.at[step], received.at[step]).wait()
        build(step)

    @pl.loop(1, dp - 1)
    def _(step):
        arrive(step)

        @pl.loop(0, parts)
        def _(part):
            add_rows(step, part, False)

    def one_feature(index, largest):
        table = left[index].T
        grad_left, hess_left = table[:NODES], table[NODES:]
        grad_total = grad_left[:, BINS - 1 :]
        hess_total = hess_left[:, BINS - 1 :]
        grad_right = grad_total - grad_left
        gains = 0.5 * (
            grad_left * grad_left / (hess_left + LAMBDA_REG)
            + grad_right * grad_right / (hess_total - hess_left + LAMBDA_REG)
            - grad_total * grad_total / (hess_total + LAMBDA_REG)
        )
        ready[:, pl.ds(index, 1), :] = gains.reshape(NODES, 1, BINS)
        return jnp.maximum(largest, jnp.maximum(gains[:, :128], gains[:, 128:]))

    def finish(part, largest):
        for u in range(group):
            largest = one_feature(part * group + u, largest)
        return largest

    def finish_and_add(part, largest):
        largest = finish(part - 1, largest)
        add_rows(dp - 1, part, False)
        return largest

    def hand_out(number, start, size):
        span = pl.ds(start, size)
        copy = pltpu.make_async_copy(
            ready.at[pl.ds(0, node_count), span], gains_ref.at[:, c, span], out_sem.at[number]
        )
        copy.start()
        outs.append(copy)
        for k in range(1, node):
            copy = pltpu.make_async_remote_copy(
                src_ref=ready.at[pl.ds(k * node_count, node_count), span],
                dst_ref=gains_ref.at[:, c, span],
                send_sem=send_out.at[number, k],
                recv_sem=recv_out.at[number, k],
                device_id={"node": (c + k) % node},
                device_id_type=MESH,
            )
            copy.start()
            copies.append(copy)

    outs = []
    early = (half - group) // 8 * 8
    largest = jnp.full((NODES, 128), -jnp.inf, jnp.float32)
    arrive(dp - 1)
    add_rows(dp - 1, 0, False)
    largest = lax.fori_loop(1, parts, finish_and_add, largest)
    if early:
        hand_out(0, 0, early)
    largest = finish(parts - 1, largest)
    hand_out(1, early, half - early)

    best = jnp.max(largest.T, axis=0, keepdims=True)
    row[0, :, 0:NODES] = jnp.broadcast_to(best, (8, NODES))
    row[0, :, NODES:] = jnp.zeros((8, 128 - NODES), jnp.float32)
    sends = []
    for step in range(1, dp):
        copy = pltpu.make_async_remote_copy(
            src_ref=row.at[0],
            dst_ref=rows_dp.at[step],
            send_sem=send_dp.at[step],
            recv_sem=recv_dp.at[step],
            device_id={"dp": partner(z, step, dp)},
            device_id_type=MESH,
        )
        copy.start()
        sends.append(copy)
    best = row[0]
    for step in range(1, dp):
        sends[step - 1].wait_recv()
        best = jnp.maximum(best, rows_dp[step])
    row[1] = best
    last = []
    for number, (i, k) in enumerate(others):
        copy = pltpu.make_async_remote_copy(
            src_ref=row.at[1],
            dst_ref=rows_all.at[number],
            send_sem=send_all.at[number],
            recv_sem=recv_all.at[number],
            device_id=place(i, k),
            device_id_type=MESH,
        )
        copy.start()
        last.append(copy)
    best = best[:, :node_count]
    for number, (i, k) in enumerate(others):
        last[number].wait_recv()
        best = jnp.maximum(
            best, rows_all[number][:, k * node_count : (k + 1) * node_count]
        )
    best_ref[...] = best

    for copy in copies + sends + last:
        copy.wait_send()
    for copy in outs:
        copy.wait()
    for number, start, size in ((0, 0, early), (1, early, half - early)):
        for k in range(1, node):
            if size:
                span = pl.ds(start, size)
                pltpu.make_async_copy(
                    ready.at[pl.ds(0, node_count), span],
                    gains_ref.at[:, (c + node - k) % node, span],
                    recv_out.at[number, k],
                ).wait()


def on_device(sizes, bins, node_ids, grad, hess):
    dp, feat, node = sizes
    feature_block, row_count = bins.shape
    half = feature_block // (dp * node)
    node_count = NODES // node
    aux = jnp.stack(
        [node_ids.astype(jnp.float32), grad.astype(jnp.float32), hess.astype(jnp.float32)], 0
    )
    split = bins.reshape(dp, node, half, row_count)
    peers = max(feat * node - 1, 1)
    dma = pltpu.SemaphoreType.DMA
    gains, best = pl.pallas_call(
        functools.partial(kernel, sizes),
        out_shape=(
            jax.ShapeDtypeStruct((node_count, node, half, BINS), jnp.float32),
            jax.ShapeDtypeStruct((8, node_count), jnp.float32),
        ),
        in_specs=[pl.BlockSpec(memory_space=pltpu.HBM), pl.BlockSpec(memory_space=pl.ANY)],
        out_specs=(
            pl.BlockSpec(memory_space=pl.ANY),
            pl.BlockSpec(memory_space=pltpu.VMEM),
        ),
        scratch_shapes=[
            pltpu.VMEM((dp, half, row_count), jnp.int32),
            pltpu.VMEM((dp, 3, row_count), jnp.float32),
            pltpu.VMEM((row_count, 2 * NODES), jnp.bfloat16),
            pltpu.VMEM((half, BINS, 2 * NODES), jnp.float32),
            pltpu.VMEM((NODES, half, BINS), jnp.float32),
            pltpu.VMEM((2, 8, 128), jnp.float32),
            pltpu.VMEM((dp, 8, 128), jnp.float32),
            pltpu.VMEM((peers, 8, 128), jnp.float32),
            dma((2,)),
            dma((dp,)), dma((dp,)), dma((dp,)), dma((dp,)),
            dma((2,)), dma((2, node)), dma((2, node)),
            dma((dp,)), dma((dp,)), dma((peers,)), dma((peers,)),
        ],
        compiler_params=pltpu.CompilerParams(
            collective_id=0, has_side_effects=True, vmem_limit_bytes=40 * 2**20
        ),
        name="split_gains",
    )(split, aux)
    return gains.reshape(node_count, node * half, BINS), best[0]


def solution(mesh):
    sizes = tuple(mesh.shape[axis] for axis in ("dp", "feat", "node"))
    return jax.shard_map(
        functools.partial(on_device, sizes),
        mesh=mesh,
        in_specs=(
            P("feat", ("groups", "dp")),
            P(("groups", "dp")),
            P(("groups", "dp")),
            P(("groups", "dp")),
        ),
        out_specs=(P(("groups", "node"), ("feat", "dp"), None), P(("groups", "node"))),
        check_vma=False,
    )
```
